32 devices in a mesh: groups: 2 (over y), region: 4 (over z), strip: 2 (over x), chan: 2 (over core).
Axes of the slice: x: 2, y: 2, z: 4, core: 2. Of those that a mesh axis runs over, the one named last changes fastest.
Arguments:
- features: bfloat16 [128, 32, 512], P(('groups', 'region', 'strip'), 'chan'), parts along dimension 0, may hold values from -6 to 6
- out_grad: bfloat16 [128, 32, 512], P(('groups', 'region', 'strip'), 'chan'), parts along dimension 0, may hold values from -6 to 6
- weight: bfloat16 [27, 32, 32], P(None, 'chan'), may hold values from -0.21875 to 0.21875
- occupancy: int32 [128, 512], P(('groups', 'region', 'strip')), parts along dimension 0, may hold values from 0 to 1, as said below
- neighbours: int32 [128, 27], P(('groups', 'region', 'strip')), parts along dimension 0, may hold values from -1 to 63, as said below
Outputs:
- grad_features: bfloat16 [128, 32, 512], P(('groups', 'region', 'strip'), 'chan'), parts along dimension 0
- grad_weight: float32 [54, 32, 32], P('groups', 'chan'), parts along dimension 0
The draws below stay inside these ranges and needn't reach their ends.
There are 2 independent parts, one for each index of `groups`. The reference program is written for one: setup_inputs(seed, part) draws one part's arguments, and reference() takes and returns one part's arrays. A program takes and returns all parts, laid end to end along the dimension named above; an argument that names none is the same for every part. Nothing has to cross between parts.
Inputs may be any that keep to these rules, and one draw needn't show every extreme that they name: `occupancy`: each brick has a level of 0 to 4, and each of its 512 voxels is occupied with probability level/4, independently; so some bricks are empty and some full. `neighbours`: the slots of a scene fill a box of 8 by 4 by 2 brick positions, one slot each, and entry t of a slot names the slot at its position moved by offset_t, or -1 outside the box. Slot s has brick coordinate s // 8 along the first dimension; index d of region+strip holds slots d * 8 to (d + 1) * 8 - 1. Entry 13 names the brick itself.
All inputs are finite; a program needn't handle non-finite values.
Results may differ from the reference program's by a relative error of at most 0.001.
Values may be sent and summed in bfloat16 or wider, within the bound.
A program may use at most 64 MiB of HBM per device.

```python
import math
import jax
import jax.numpy as jnp
from jax import lax

C = 32
GY = 4
GZ = 2
BX = 1
NF = 8
NB = 8
DEVS = 8
TOTAL = 64


def draw_occupancy(key, part):
    key = jax.random.fold_in(key, 11)
    level_key, cell_key = jax.random.split(key)
    levels = jax.random.randint(level_key, (TOTAL, 1), 0, 5)
    cells = jax.random.randint(cell_key, (TOTAL, 512), 0, 4)
    return (cells < levels).astype(jnp.int32)


def draw_neighbours(key, part):
    key = jax.random.fold_in(key, 23)
    layer_count = DEVS * BX
    layer_keys = jax.random.split(key, layer_count)
    places = jax.vmap(lambda layer_key: jax.random.permutation(layer_key, NF))(layer_keys).astype(jnp.int32)
    inverse = jnp.argsort(places, axis=1).astype(jnp.int32)
    slots = jnp.arange(TOTAL, dtype=jnp.int32)
    coord_x = slots // NF
    position = places[coord_x, slots % NF]
    coord_y = position // GZ
    coord_z = position % GZ
    columns = []
    for step_x in (-1, 0, 1):
        for step_y in (-1, 0, 1):
            for step_z in (-1, 0, 1):
                next_x = coord_x + step_x
                next_y = coord_y + step_y
                next_z = coord_z + step_z
                inside = (next_x >= 0) & (next_x < layer_count) & (next_y >= 0) & (next_y < GY) & (next_z >= 0) & (next_z < GZ)
                safe_x = jnp.clip(next_x, 0, layer_count - 1)
                safe_y = jnp.clip(next_y, 0, GY - 1)
                safe_z = jnp.clip(next_z, 0, GZ - 1)
                target = safe_x * NF + inverse[safe_x, safe_y * GZ + safe_z]
                columns.append(jnp.where(inside, target, -1))
    return jnp.stack(columns, axis=1).astype(jnp.int32)


def steps_of(own_key, shape, pieces, smallest, largest):
    loudness, own = 1.0, jax.random.fold_in(own_key, 6)
    for dim, parts in pieces:
        draws = jnp.exp(jax.random.uniform(jax.random.fold_in(own, dim), (parts,), jnp.float32, smallest / len(pieces), largest / len(pieces)))
        loudness = loudness * jnp.repeat(draws, shape[dim] // parts).reshape([-1 if axis == dim else 1 for axis in range(len(shape))])
    return loudness


def centred(stream_key, dims, spread, limit, cuts=(), held_as=jnp.bfloat16):
    factor_of = steps_of(stream_key, dims, cuts, -0.22, 0.18) if cuts else 1.0
    array = jax.random.normal(stream_key, dims, jnp.float32) * spread * factor_of
    return jnp.minimum(jnp.maximum(array, -limit), limit).astype(held_as)


def setup_inputs(seed: int = 0, part: int = 0) -> dict:
    splits = jax.random.split(jax.random.key(seed), 6)
    part_splits = jax.random.split(jax.random.fold_in(splits[5], part), 6)
    features = centred(part_splits[0], (TOTAL, C, 512), 1.0, 6.0, ((0, 8), (1, 2)))
    out_grad = centred(part_splits[1], (TOTAL, C, 512), 1.0, 6.0, ((0, 8), (1, 2)))
    weight = centred(splits[2], (27, C, C), (27 * C) ** -0.5, 0.21875, ((1, 2),))
    occupancy = draw_occupancy(jax.random.fold_in(jax.random.fold_in(splits[5], part), 71), part)
    neighbours = draw_neighbours(jax.random.fold_in(jax.random.fold_in(splits[5], part), 71), part)
    return dict(features=features, out_grad=out_grad, weight=weight, occupancy=occupancy, neighbours=neighbours)


tap_offsets = [(step_x, step_y, step_z) for step_x in (-1, 0, 1) for step_y in (-1, 0, 1) for step_z in (-1, 0, 1)]

def source_range(offset_value):
    if offset_value < 0:
        return (7, 8)
    if offset_value > 0:
        return (0, 1)
    return (0, 8)

def assemble(piece):
    slabs = []
    for step_x in (-1, 0, 1):
        layers = []
        for step_y in (-1, 0, 1):
            layers.append(jnp.concatenate([piece(step_x, step_y, step_z) for step_z in (-1, 0, 1)], axis=4))
        slabs.append(jnp.concatenate(layers, axis=3))
    return jnp.concatenate(slabs, axis=2)

def reference(features, out_grad, weight, occupancy, neighbours):
    occupied = occupancy.astype(jnp.bfloat16)
    masked_x = features * occupied[:, None, :]
    masked_g = out_grad * occupied[:, None, :]
    cube_x = masked_x.reshape(TOTAL, C, 8, 8, 8)
    cube_g = masked_g.reshape(TOTAL, C, 8, 8, 8)
    weight_full = weight.astype(jnp.float32)

    def one_block(operands):
        block_links, block_grad, block_mask = operands

        def padded(cube):

            def piece(step_x, step_y, step_z):
                tap_index = 9 * (step_x + 1) + 3 * (step_y + 1) + (step_z + 1)
                column = block_links[:, tap_index]
                x_low, x_high = source_range(step_x)
                y_low, y_high = source_range(step_y)
                z_low, z_high = source_range(step_z)
                taken = cube[jnp.maximum(column, 0)][:, :, x_low:x_high, y_low:y_high, z_low:z_high]
                return jnp.where((column >= 0)[:, None, None, None, None], taken, jnp.zeros_like(taken))
            return assemble(piece)
        padded_x = padded(cube_x)
        padded_g = padded(cube_g)
        grad_rows = jnp.zeros((NB, C, 512), jnp.float32)
        weight_terms = []
        for tap_index, (step_x, step_y, step_z) in enumerate(tap_offsets):
            window_g = padded_g[:, :, 1 - step_x:9 - step_x, 1 - step_y:9 - step_y, 1 - step_z:9 - step_z].reshape(NB, C, 512)
            grad_rows = grad_rows + jnp.einsum('io,bop->bip', weight_full[tap_index], window_g.astype(jnp.float32))
            window_x = padded_x[:, :, 1 + step_x:9 + step_x, 1 + step_y:9 + step_y, 1 + step_z:9 + step_z].reshape(NB, C, 512)
            weight_terms.append(jnp.einsum('bip,bop->io', window_x.astype(jnp.float32), block_grad.astype(jnp.float32)))
        grad_rows = grad_rows * block_mask.astype(jnp.float32)[:, None, :]
        return (grad_rows.astype(jnp.bfloat16), jnp.stack(weight_terms))
    grad_blocks, term_blocks = lax.map(one_block, (neighbours.reshape(DEVS, NB, 27), masked_g.reshape(DEVS, NB, C, 512), occupancy.reshape(DEVS, NB, 512)))
    grad_features = grad_blocks.reshape(TOTAL, C, 512)
    grad_weight = lax.optimization_barrier(jnp.sum(term_blocks, axis=0)) * (1.0 / math.sqrt(TOTAL * 512))
    return (grad_features, grad_weight)
```

```python
import math

import jax
import jax.numpy as jnp
from jax import lax
from jax.experimental import pallas as pl
from jax.experimental.pallas import tpu as pltpu
from jax.sharding import PartitionSpec as P

GY = 4
GZ = 2
BRICKS = GY * GZ
EDGE = 8
LANES = 512
PARTS = 6
MESH = pl.DeviceIdType.MESH
LINE = ("region", "strip")


def lane_of(shape):
    return lax.broadcasted_iota(jnp.int32, shape, len(shape) - 1)


def roll(a, distance):
    return pltpu.roll(a, distance % LANES, 1)


def at_y(a, step):
    lane = lane_of(a.shape)
    row = (lane // 8) % 8
    brick = lane // 128
    if step > 0:
        near, far, other = row < 7, brick < GY - 1, 72
    else:
        near, far, other = row > 0, brick > 0, 72
    return jnp.where(
        near,
        roll(a, -8 * step),
        jnp.where(far, roll(a, -other * step), jnp.zeros_like(a)),
    )


def at_z(a, step):
    lane = lane_of(a.shape)
    column = lane % 8
    brick = (lane // 64) % 2
    if step > 0:
        near, far = column < 7, brick == 0
    else:
        near, far = column > 0, brick == 1
    return jnp.where(
        near,
        roll(a, -step),
        jnp.where(far, roll(a, -57 * step), jnp.zeros_like(a)),
    )


def planes_of(first, second):
    low = lane_of(first.shape) % 128 < 64
    even = jnp.where(low, first, roll(second, 64))
    odd = jnp.where(low, roll(first, -64), second)
    return even, odd


def kernel(
    scale,
    f_ref,
    g_ref,
    w_ref,
    occ_ref,
    nb_ref,
    gf_ref,
    gw_ref,
    grads,
    masked,
    feats,
    shifted,
    weights,
    rows,
    terms,
    arrived,
    totals,
    face_send,
    face_recv,
    part_send,
    part_recv,
    total_send,
    total_recv,
):
    strips = lax.axis_size("strip")
    count = strips * lax.axis_size("region")
    chan = lax.axis_index("chan")
    me = lax.axis_index("region") * strips + lax.axis_index("strip")
    other = 1 - chan

    def place(index, core):
        return {
            "region": lax.div(index, strips),
            "strip": lax.rem(index, strips),
            "chan": core,
        }

    def each_peer(body):
        if count <= 8:
            for j in range(1, count):
                body(lax.rem(me + j, count), j)
        else:

            def step(j, carry):
                body(lax.rem(me + j, count), j)
                return carry

            lax.fori_loop(1, count, step, 0)

    barrier = pltpu.get_barrier_semaphore()

    def greet(index, core):
        pl.semaphore_signal(
            barrier, inc=1, device_id=place(index, core), device_id_type=MESH
        )

    greet(me, other)

    @pl.when(me > 0)
    def _():
        greet(me - 1, other)

    @pl.when(me < count - 1)
    def _():
        greet(me + 1, other)

    each_peer(lambda peer, j: greet(peer, chan))

    base = me * BRICKS

    def own(entry):
        return jnp.clip(entry - base, 0, BRICKS - 1)

    corner = 0
    for b in range(BRICKS):
        corner += jnp.where((nb_ref[b, 10] < 0) & (nb_ref[b, 12] < 0), b, 0)
    slots = []
    here = corner
    for by in range(GY):
        slots.append((here, own(nb_ref[here, 14])))
        if by < GY - 1:
            here = own(nb_ref[here, 16])

    for b in range(BRICKS):
        occupied = occ_ref[b : b + 1, :].astype(jnp.float32)
        masked[b] = g_ref[b].astype(jnp.float32) * occupied
    for by in range(GY):
        even, odd = planes_of(masked[slots[by][0]], masked[slots[by][1]])
        at = slice(128 * by, 128 * (by + 1))
        for k in range(4):
            part = slice(128 * k, 128 * (k + 1))
            grads[1 + 2 * k, chan, :, at] = even[:, part].astype(jnp.bfloat16)
            grads[2 + 2 * k, chan, :, at] = odd[:, part].astype(jnp.bfloat16)

    zero_plane = jnp.zeros((2, 16, LANES), jnp.bfloat16)

    @pl.when(me == 0)
    def _():
        grads[0] = zero_plane

    @pl.when(me == count - 1)
    def _():
        grads[EDGE + 1] = zero_plane

    neighbours = 2 + (me > 0).astype(jnp.int32) + (me < count - 1).astype(jnp.int32)
    pl.semaphore_wait(barrier, count - 2 + neighbours)

    def send_plane(source, target, index, core, k, channel):
        return pltpu.make_async_remote_copy(
            src_ref=grads.at[source, channel],
            dst_ref=grads.at[target, channel],
            send_sem=face_send.at[k],
            recv_sem=face_recv.at[k],
            device_id=place(index, core),
            device_id_type=MESH,
        )

    to_next = [
        send_plane(EDGE, 0, me + 1, chan, 1, chan),
        send_plane(EDGE, 0, me + 1, other, 2, chan),
    ]
    to_last = [
        send_plane(1, EDGE + 1, me - 1, chan, 3, chan),
        send_plane(1, EDGE + 1, me - 1, other, 4, chan),
    ]
    from_last = [
        send_plane(EDGE, 0, me - 1, chan, 1, chan),
        send_plane(EDGE, 0, me - 1, other, 2, other),
    ]
    from_next = [
        send_plane(1, EDGE + 1, me + 1, chan, 3, chan),
        send_plane(1, EDGE + 1, me + 1, other, 4, other),
    ]

    @pl.when(me < count - 1)
    def _():
        for copy in to_next:
            copy.start()

    @pl.when(me > 0)
    def _():
        for copy in to_last:
            copy.start()

    swap = send_plane(pl.ds(1, EDGE), pl.ds(1, EDGE), me, other, 0, chan)
    swap.start()
    swap_in = send_plane(pl.ds(1, EDGE), pl.ds(1, EDGE), me, other, 0, other)

    for b in range(BRICKS):
        occupied = occ_ref[b : b + 1, :].astype(jnp.float32)
        masked[b] = f_ref[b].astype(jnp.float32) * occupied
    for by in range(GY):
        even, odd = planes_of(masked[slots[by][0]], masked[slots[by][1]])
        at = slice(128 * by, 128 * (by + 1))
        for k in range(4):
            part = slice(128 * k, 128 * (k + 1))
            feats[2 * k, :, at] = even[:, part]
            feats[2 * k + 1, :, at] = odd[:, part]
    for x in range(EDGE):
        plane = feats[x]
        depth = jnp.concatenate([at_z(plane, -1), plane, at_z(plane, 1)], axis=0)
        shifted[x, 0:48] = at_y(depth, -1).astype(jnp.bfloat16)
        shifted[x, 48:96] = depth.astype(jnp.bfloat16)
        shifted[x, 96:144] = at_y(depth, 1).astype(jnp.bfloat16)
    for a in range(3):
        weights[:, 32 * a : 32 * (a + 1)] = w_ref[9 * a : 9 * (a + 1)].reshape(144, 32)

    def window(x):
        return jnp.concatenate(
            [grads[x + 2 - a].reshape(32, LANES) for a in range(3)], axis=0
        )

    def term(x):
        return lax.dot_general(
            shifted[x],
            window(x),
            (((1,), (1,)), ((), ())),
            preferred_element_type=jnp.float32,
        )

    swap_in.wait_recv()
    total = term(1)
    for x in range(2, EDGE - 1):
        total = total + term(x)

    @pl.when(me > 0)
    def _():
        for copy in from_last:
            copy.wait_recv()

    @pl.when(me < count - 1)
    def _():
        for copy in from_next:
            copy.wait_recv()

    total = total + term(0) + term(EDGE - 1)
    terms[...] = total.reshape(terms.shape)

    def give(q, source):
        return pltpu.make_async_remote_copy(
            src_ref=terms.at[q],
            dst_ref=arrived.at[source],
            send_sem=part_send.at[q],
            recv_sem=part_recv.at[source],
            device_id=place(q, chan),
            device_id_type=MESH,
        )

    for q in range(PARTS):

        @pl.when(me != q)
        def _():
            give(q, me).start()

    for x in range(EDGE):
        taps = jnp.dot(weights[...], window(x), preferred_element_type=jnp.float32)
        depth = taps[48:96] + at_y(taps[0:48], 1) + at_y(taps[96:144], -1)
        feats[x] = depth[16:32] + at_z(depth[0:16], 1) + at_z(depth[32:48], -1)
    for by in range(GY):
        at = slice(128 * by, 128 * (by + 1))
        even = jnp.concatenate([feats[2 * k, :, at] for k in range(4)], axis=1)
        odd = jnp.concatenate([feats[2 * k + 1, :, at] for k in range(4)], axis=1)
        first, second = planes_of(even, odd)
        rows[GZ * by] = first
        rows[GZ * by + 1] = second
    for b in range(BRICKS):
        below = nb_ref[b, 10]
        two_below = nb_ref[own(below), 10]
        y = jnp.where(
            below < 0,
            0,
            jnp.where(two_below < 0, 1, jnp.where(nb_ref[b, 16] >= 0, 2, 3)),
        )
        z = jnp.where(nb_ref[b, 12] >= 0, 1, 0)
        occupied = occ_ref[b : b + 1, :].astype(jnp.float32)
        gf_ref[b] = (rows[GZ * y + z] * occupied).astype(jnp.bfloat16)

    def share(owner, target):
        return pltpu.make_async_remote_copy(
            src_ref=totals.at[owner],
            dst_ref=totals.at[owner],
            send_sem=total_send.at[target],
            recv_sem=total_recv.at[owner],
            device_id=place(target, chan),
            device_id_type=MESH,
        )

    @pl.when(me < PARTS)
    def _():
        each_peer(lambda peer, j: give(me, peer).wait_recv())
        arrived[me] = terms[me]

        def add(j, carry):
            return carry + arrived[j]

        if count <= 8:
            result = arrived[0]
            for j in range(1, count):
                result = add(j, result)
        else:
            result = lax.fori_loop(1, count, add, arrived[0])
        totals[me] = result * scale
        each_peer(lambda peer, j: share(me, peer).start())

    for q in range(PARTS):

        @pl.when(me != q)
        def _():
            share(q, q).wait_recv()

    whole = totals[...].reshape(144, 96)
    for a in range(3):
        gw_ref[9 * a : 9 * (a + 1)] = whole[:, 32 * a : 32 * (a + 1)].reshape(9, 16, 32)

    @pl.when(me < PARTS)
    def _():
        each_peer(lambda peer, j: share(me, peer).wait_send())

    for q in range(PARTS):

        @pl.when(me != q)
        def _():
            give(q, me).wait_send()

    swap.wait_send()

    @pl.when(me < count - 1)
    def _():
        for copy in to_next:
            copy.wait_send()

    @pl.when(me > 0)
    def _():
        for copy in to_last:
            copy.wait_send()


def local(features, out_grad, weight, occupancy, neighbours):
    count = lax.axis_size(LINE)
    scale = 1.0 / math.sqrt(features.shape[0] * count * LANES)
    part = (24, 96)
    vmem = pl.BlockSpec(memory_space=pltpu.VMEM)

    def body(*refs):
        kernel(scale, *refs)

    return pl.pallas_call(
        body,
        out_shape=(
            jax.ShapeDtypeStruct(features.shape, jnp.bfloat16),
            jax.ShapeDtypeStruct(weight.shape, jnp.float32),
        ),
        in_specs=[vmem, vmem, vmem, vmem, pl.BlockSpec(memory_space=pltpu.SMEM)],
        out_specs=(vmem, vmem),
        scratch_shapes=[
            pltpu.VMEM((EDGE + 2, 2, 16, LANES), jnp.bfloat16),
            pltpu.VMEM((BRICKS, 16, LANES), jnp.float32),
            pltpu.VMEM((EDGE, 16, LANES), jnp.float32),
            pltpu.VMEM((EDGE, 144, LANES), jnp.bfloat16),
            pltpu.VMEM((144, 96), jnp.bfloat16),
            pltpu.VMEM((BRICKS, 16, LANES), jnp.float32),
            pltpu.VMEM((PARTS,) + part, jnp.float32),
            pltpu.VMEM((count,) + part, jnp.float32),
            pltpu.VMEM((PARTS,) + part, jnp.float32),
            pltpu.SemaphoreType.DMA((5,)),
            pltpu.SemaphoreType.DMA((5,)),
            pltpu.SemaphoreType.DMA((PARTS,)),
            pltpu.SemaphoreType.DMA((count,)),
            pltpu.SemaphoreType.DMA((count,)),
            pltpu.SemaphoreType.DMA((PARTS,)),
        ],
        compiler_params=pltpu.CompilerParams(
            collective_id=0, has_side_effects=True, vmem_limit_bytes=32 * 1024 * 1024
        ),
        name="brick_conv_backward",
    )(features, out_grad, weight, occupancy, neighbours)


def solution(mesh):
    rows = P(("groups", "region", "strip"), "chan", None)
    tables = P(("groups", "region", "strip"), None)
    return jax.shard_map(
        local,
        mesh=mesh,
        in_specs=(rows, rows, P(None, "chan", None), tables, tables),
        out_specs=(rows, P("groups", "chan", None)),
        check_vma=False,
    )
```

```python
import math

import jax
import jax.numpy as jnp
from jax import lax
from jax.experimental import pallas as pl
from jax.experimental.pallas import tpu as pltpu
from jax.sharding import PartitionSpec as P

GY = 4
GZ = 2
BRICKS = GY * GZ
EDGE = 8
LANES = 512
PARTS = 6
MESH = pl.DeviceIdType.MESH
LINE = ("region", "strip")


def lane_of(shape):
    return lax.broadcasted_iota(jnp.int32, shape, len(shape) - 1)


def roll(a, distance):
    return pltpu.roll(a, distance % LANES, 1)


def at_y(a, step):
    lane = lane_of(a.shape)
    row = (lane // 8) % 8
    brick = lane // 128
    if step > 0:
        near, far, other = row < 7, brick < GY - 1, 72
    else:
        near, far, other = row > 0, brick > 0, 72
    return jnp.where(
        near,
        roll(a, -8 * step),
        jnp.where(far, roll(a, -other * step), jnp.zeros_like(a)),
    )


def at_z(a, step):
    lane = lane_of(a.shape)
    column = lane % 8
    brick = (lane // 64) % 2
    if step > 0:
        near, far = column < 7, brick == 0
    else:
        near, far = column > 0, brick == 1
    return jnp.where(
        near,
        roll(a, -step),
        jnp.where(far, roll(a, -57 * step), jnp.zeros_like(a)),
    )


def planes_of(first, second):
    low = lane_of(first.shape) % 128 < 64
    even = jnp.where(low, first, roll(second, 64))
    odd = jnp.where(low, roll(first, -64), second)
    return even, odd


def kernel(
    scale,
    f_in,
    g_in,
    w_in,
    occ_in,
    nb_in,
    gf_ref,
    gw_ref,
    f_ref,
    g_ref,
    w_ref,
    occ_ref,
    nb_ref,
    load_sem,
    grads,
    masked,
    feats,
    shifted,
    weights,
    rows,
    terms,
    arrived,
    totals,
    face_send,
    face_recv,
    part_send,
    part_recv,
    total_send,
    total_recv,
):
    strips = lax.axis_size("strip")
    count = strips * lax.axis_size("region")
    chan = lax.axis_index("chan")
    me = lax.axis_index("region") * strips + lax.axis_index("strip")
    other = 1 - chan

    def place(index, core):
        return {
            "region": lax.div(index, strips),
            "strip": lax.rem(index, strips),
            "chan": core,
        }

    def each_peer(body):
        if count <= 8:
            for j in range(1, count):
                body(lax.rem(me + j, count), j)
        else:

            def step(j, carry):
                body(lax.rem(me + j, count), j)
                return carry

            lax.fori_loop(1, count, step, 0)

    pairs = (
        (nb_in, nb_ref),
        (occ_in, occ_ref),
        (g_in, g_ref),
        (f_in, f_ref),
        (w_in, w_ref),
    )
    loads = [
        pltpu.make_async_copy(source, target, load_sem.at[k])
        for k, (source, target) in enumerate(pairs)
    ]
    for load in loads:
        load.start()

    barrier = pltpu.get_barrier_semaphore()

    def greet(index, core):
        pl.semaphore_signal(
            barrier, inc=1, device_id=place(index, core), device_id_type=MESH
        )

    greet(me, other)

    @pl.when(me > 0)
    def _():
        greet(me - 1, other)

    @pl.when(me < count - 1)
    def _():
        greet(me + 1, other)

    each_peer(lambda peer, j: greet(peer, chan))

    base = me * BRICKS

    def own(entry):
        return jnp.clip(entry - base, 0, BRICKS - 1)

    loads[0].wait()
    corner = 0
    for b in range(BRICKS):
        corner += jnp.where((nb_ref[b, 10] < 0) & (nb_ref[b, 12] < 0), b, 0)
    slots = []
    here = corner
    for by in range(GY):
        slots.append((here, own(nb_ref[here, 14])))
        if by < GY - 1:
            here = own(nb_ref[here, 16])

    loads[1].wait()
    loads[2].wait()
    for b in range(BRICKS):
        occupied = occ_ref[b : b + 1, :].astype(jnp.float32)
        masked[b] = g_ref[b].astype(jnp.float32) * occupied
    for by in range(GY):
        even, odd = planes_of(masked[slots[by][0]], masked[slots[by][1]])
        at = slice(128 * by, 128 * (by + 1))
        for k in range(4):
            part = slice(128 * k, 128 * (k + 1))
            grads[1 + 2 * k, chan, :, at] = even[:, part].astype(jnp.bfloat16)
            grads[2 + 2 * k, chan, :, at] = odd[:, part].astype(jnp.bfloat16)

    zero_plane = jnp.zeros((2, 16, LANES), jnp.bfloat16)

    @pl.when(me == 0)
    def _():
        grads[0] = zero_plane

    @pl.when(me == count - 1)
    def _():
        grads[EDGE + 1] = zero_plane

    neighbours = 2 + (me > 0).astype(jnp.int32) + (me < count - 1).astype(jnp.int32)
    pl.semaphore_wait(barrier, count - 2 + neighbours)

    def send_plane(source, target, index, core, k, channel):
        return pltpu.make_async_remote_copy(
            src_ref=grads.at[source, channel],
            dst_ref=grads.at[target, channel],
            send_sem=face_send.at[k],
            recv_sem=face_recv.at[k],
            device_id=place(index, core),
            device_id_type=MESH,
        )

    to_next = [
        send_plane(EDGE, 0, me + 1, chan, 1, chan),
        send_plane(EDGE, 0, me + 1, other, 2, chan),
    ]
    to_last = [
        send_plane(1, EDGE + 1, me - 1, chan, 3, chan),
        send_plane(1, EDGE + 1, me - 1, other, 4, chan),
    ]
    from_last = [
        send_plane(EDGE, 0, me - 1, chan, 1, chan),
        send_plane(EDGE, 0, me - 1, other, 2, other),
    ]
    from_next = [
        send_plane(1, EDGE + 1, me + 1, chan, 3, chan),
        send_plane(1, EDGE + 1, me + 1, other, 4, other),
    ]

    @pl.when(me < count - 1)
    def _():
        for copy in to_next:
            copy.start()

    @pl.when(me > 0)
    def _():
        for copy in to_last:
            copy.start()

    swap = send_plane(pl.ds(1, EDGE), pl.ds(1, EDGE), me, other, 0, chan)
    swap.start()
    swap_in = send_plane(pl.ds(1, EDGE), pl.ds(1, EDGE), me, other, 0, other)

    loads[3].wait()
    for b in range(BRICKS):
        occupied = occ_ref[b : b + 1, :].astype(jnp.float32)
        masked[b] = f_ref[b].astype(jnp.float32) * occupied
    for by in range(GY):
        even, odd = planes_of(masked[slots[by][0]], masked[slots[by][1]])
        at = slice(128 * by, 128 * (by + 1))
        for k in range(4):
            part = slice(128 * k, 128 * (k + 1))
            feats[2 * k, :, at] = even[:, part]
            feats[2 * k + 1, :, at] = odd[:, part]
    for x in range(EDGE):
        plane = feats[x]
        depth = jnp.concatenate([at_z(plane, -1), plane, at_z(plane, 1)], axis=0)
        shifted[x, 0:48] = at_y(depth, -1).astype(jnp.bfloat16)
        shifted[x, 48:96] = depth.astype(jnp.bfloat16)
        shifted[x, 96:144] = at_y(depth, 1).astype(jnp.bfloat16)
    loads[4].wait()
    for a in range(3):
        weights[:, 32 * a : 32 * (a + 1)] = w_ref[9 * a : 9 * (a + 1)].reshape(144, 32)

    def window(x):
        return jnp.concatenate(
            [grads[x + 2 - a].reshape(32, LANES) for a in range(3)], axis=0
        )

    def term(x):
        return lax.dot_general(
            shifted[x],
            window(x),
            (((1,), (1,)), ((), ())),
            preferred_element_type=jnp.float32,
        )

    swap_in.wait_recv()
    total = term(1)
    for x in range(2, EDGE - 1):
        total = total + term(x)

    @pl.when(me > 0)
    def _():
        for copy in from_last:
            copy.wait_recv()

    @pl.when(me < count - 1)
    def _():
        for copy in from_next:
            copy.wait_recv()

    total = total + term(0) + term(EDGE - 1)
    terms[...] = total.reshape(terms.shape)

    def give(q, source):
        return pltpu.make_async_remote_copy(
            src_ref=terms.at[q],
            dst_ref=arrived.at[source],
            send_sem=part_send.at[q],
            recv_sem=part_recv.at[source],
            device_id=place(q, chan),
            device_id_type=MESH,
        )

    for q in range(PARTS):

        @pl.when(me != q)
        def _():
            give(q, me).start()

    for x in range(EDGE):
        taps = jnp.dot(weights[...], window(x), preferred_element_type=jnp.float32)
        depth = taps[48:96] + at_y(taps[0:48], 1) + at_y(taps[96:144], -1)
        feats[x] = depth[16:32] + at_z(depth[0:16], 1) + at_z(depth[32:48], -1)
    for by in range(GY):
        at = slice(128 * by, 128 * (by + 1))
        even = jnp.concatenate([feats[2 * k, :, at] for k in range(4)], axis=1)
        odd = jnp.concatenate([feats[2 * k + 1, :, at] for k in range(4)], axis=1)
        first, second = planes_of(even, odd)
        rows[GZ * by] = first
        rows[GZ * by + 1] = second
    for b in range(BRICKS):
        below = nb_ref[b, 10]
        two_below = nb_ref[own(below), 10]
        y = jnp.where(
            below < 0,
            0,
            jnp.where(two_below < 0, 1, jnp.where(nb_ref[b, 16] >= 0, 2, 3)),
        )
        z = jnp.where(nb_ref[b, 12] >= 0, 1, 0)
        occupied = occ_ref[b : b + 1, :].astype(jnp.float32)
        gf_ref[b] = (rows[GZ * y + z] * occupied).astype(jnp.bfloat16)

    def share(owner, target):
        return pltpu.make_async_remote_copy(
            src_ref=totals.at[owner],
            dst_ref=totals.at[owner],
            send_sem=total_send.at[target],
            recv_sem=total_recv.at[owner],
            device_id=place(target, chan),
            device_id_type=MESH,
        )

    @pl.when(me < PARTS)
    def _():
        each_peer(lambda peer, j: give(me, peer).wait_recv())
        arrived[me] = terms[me]

        def add(j, carry):
            return carry + arrived[j]

        if count <= 8:
            result = arrived[0]
            for j in range(1, count):
                result = add(j, result)
        else:
            result = lax.fori_loop(1, count, add, arrived[0])
        totals[me] = result * scale
        each_peer(lambda peer, j: share(me, peer).start())

    for q in range(PARTS):

        @pl.when(me != q)
        def _():
            share(q, q).wait_recv()

    whole = totals[...].reshape(144, 96)
    for a in range(3):
        gw_ref[9 * a : 9 * (a + 1)] = whole[:, 32 * a : 32 * (a + 1)].reshape(9, 16, 32)

    @pl.when(me < PARTS)
    def _():
        each_peer(lambda peer, j: share(me, peer).wait_send())

    for q in range(PARTS):

        @pl.when(me != q)
        def _():
            give(q, me).wait_send()

    swap.wait_send()

    @pl.when(me < count - 1)
    def _():
        for copy in to_next:
            copy.wait_send()

    @pl.when(me > 0)
    def _():
        for copy in to_last:
            copy.wait_send()


def local(features, out_grad, weight, occupancy, neighbours):
    count = lax.axis_size(LINE)
    scale = 1.0 / math.sqrt(features.shape[0] * count * LANES)
    part = (24, 96)
    vmem = pl.BlockSpec(memory_space=pltpu.VMEM)

    def body(*refs):
        kernel(scale, *refs)

    return pl.pallas_call(
        body,
        out_shape=(
            jax.ShapeDtypeStruct(features.shape, jnp.bfloat16),
            jax.ShapeDtypeStruct(weight.shape, jnp.float32),
        ),
        in_specs=[pl.BlockSpec(memory_space=pltpu.HBM)] * 5,
        out_specs=(vmem, vmem),
        scratch_shapes=[
            pltpu.VMEM(features.shape, jnp.bfloat16),
            pltpu.VMEM(out_grad.shape, jnp.bfloat16),
            pltpu.VMEM(weight.shape, jnp.bfloat16),
            pltpu.VMEM(occupancy.shape, jnp.int32),
            pltpu.SMEM(neighbours.shape, jnp.int32),
            pltpu.SemaphoreType.DMA((5,)),
            pltpu.VMEM((EDGE + 2, 2, 16, LANES), jnp.bfloat16),
            pltpu.VMEM((BRICKS, 16, LANES), jnp.float32),
            pltpu.VMEM((EDGE, 16, LANES), jnp.float32),
            pltpu.VMEM((EDGE, 144, LANES), jnp.bfloat16),
            pltpu.VMEM((144, 96), jnp.bfloat16),
            pltpu.VMEM((BRICKS, 16, LANES), jnp.float32),
            pltpu.VMEM((PARTS,) + part, jnp.float32),
            pltpu.VMEM((count,) + part, jnp.float32),
            pltpu.VMEM((PARTS,) + part, jnp.float32),
            pltpu.SemaphoreType.DMA((5,)),
            pltpu.SemaphoreType.DMA((5,)),
            pltpu.SemaphoreType.DMA((PARTS,)),
            pltpu.SemaphoreType.DMA((count,)),
            pltpu.SemaphoreType.DMA((count,)),
            pltpu.SemaphoreType.DMA((PARTS,)),
        ],
        compiler_params=pltpu.CompilerParams(
            collective_id=0, has_side_effects=True, vmem_limit_bytes=60 * 1024 * 1024
        ),
        name="brick_conv_backward",
    )(features, out_grad, weight, occupancy, neighbours)


def solution(mesh):
    rows = P(("groups", "region", "strip"), "chan", None)
    tables = P(("groups", "region", "strip"), None)
    return jax.shard_map(
        local,
        mesh=mesh,
        in_specs=(rows, rows, P(None, "chan", None), tables, tables),
        out_specs=(rows, P("groups", "chan", None)),
        check_vma=False,
    )
```

```python
import math

import jax
import jax.numpy as jnp
from jax import lax
from jax.experimental import pallas as pl
from jax.experimental.pallas import tpu as pltpu
from jax.sharding import PartitionSpec as P

GY = 4
GZ = 2
BRICKS = GY * GZ
EDGE = 8
LANES = 512
PARTS = 4
PART_ROWS = 40
MESH = pl.DeviceIdType.MESH
LINE = ("region", "strip")


def lane_of(shape):
    return lax.broadcasted_iota(jnp.int32, shape, len(shape) - 1)


def roll(a, distance):
    return pltpu.roll(a, distance % LANES, 1)


def at_y(a, step):
    lane = lane_of(a.shape)
    row = (lane // 8) % 8
    brick = lane // 128
    if step > 0:
        near, far, other = row < 7, brick < GY - 1, 72
    else:
        near, far, other = row > 0, brick > 0, 72
    return jnp.where(
        near,
        roll(a, -8 * step),
        jnp.where(far, roll(a, -other * step), jnp.zeros_like(a)),
    )


def at_z(a, step):
    lane = lane_of(a.shape)
    column = lane % 8
    brick = (lane // 64) % 2
    if step > 0:
        near, far = column < 7, brick == 0
    else:
        near, far = column > 0, brick == 1
    return jnp.where(
        near,
        roll(a, -step),
        jnp.where(far, roll(a, -57 * step), jnp.zeros_like(a)),
    )


def planes_of(first, second):
    low = lane_of(first.shape) % 128 < 64
    even = jnp.where(low, first, roll(second, 64))
    odd = jnp.where(low, roll(first, -64), second)
    return even, odd


def kernel(
    scale,
    f_in,
    g_in,
    w_in,
    occ_in,
    nb_in,
    gf_out,
    gw_out,
    gf_ref,
    gw_ref,
    store_sem,
    f_ref,
    g_ref,
    w_ref,
    occ_ref,
    nb_ref,
    load_sem,
    grads,
    masked,
    feats,
    shifted,
    weights,
    rows,
    terms,
    arrived,
    totals,
    face_send,
    face_recv,
    part_send,
    part_recv,
    total_send,
    total_recv,
):
    strips = lax.axis_size("strip")
    count = strips * lax.axis_size("region")
    chan = lax.axis_index("chan")
    me = lax.axis_index("region") * strips + lax.axis_index("strip")
    other = 1 - chan
    first = (count - PARTS) // 2

    def owns(index):
        return (index >= first) & (index < first + PARTS)

    def place(index, core):
        return {
            "region": lax.div(index, strips),
            "strip": lax.rem(index, strips),
            "chan": core,
        }

    def each_peer(body):
        if count <= 8:
            for j in range(1, count):
                body(lax.rem(me + j, count), j)
        else:

            def step(j, carry):
                body(lax.rem(me + j, count), j)
                return carry

            lax.fori_loop(1, count, step, 0)

    barrier = pltpu.get_barrier_semaphore()

    def greet(index, core):
        pl.semaphore_signal(
            barrier, inc=1, device_id=place(index, core), device_id_type=MESH
        )

    below, above = me > 0, me < count - 1
    plain = jnp.logical_not(owns(me))
    meet_below = below & plain & jnp.logical_not(owns(me - 1))
    meet_above = above & plain & jnp.logical_not(owns(me + 1))

    @pl.when(owns(me))
    def _():
        each_peer(lambda peer, j: greet(peer, chan))

    @pl.when(plain)
    def _():
        for q in range(PARTS):
            greet(first + q, chan)

    @pl.when(meet_below)
    def _():
        greet(me - 1, chan)

    @pl.when(meet_above)
    def _():
        greet(me + 1, chan)

    @pl.when(below)
    def _():
        greet(me - 1, other)

    @pl.when(above)
    def _():
        greet(me + 1, other)

    greet(me, other)

    pairs = (
        (nb_in, nb_ref),
        (occ_in, occ_ref),
        (g_in, g_ref),
        (f_in, f_ref),
        (w_in, w_ref),
    )
    loads = [
        pltpu.make_async_copy(source, target, load_sem.at[k])
        for k, (source, target) in enumerate(pairs)
    ]
    for load in loads:
        load.start()

    base = me * BRICKS

    def own(entry):
        return jnp.clip(entry - base, 0, BRICKS - 1)

    loads[0].wait()
    corner = 0
    for b in range(BRICKS):
        corner += jnp.where((nb_ref[b, 10] < 0) & (nb_ref[b, 12] < 0), b, 0)
    slots = []
    here = corner
    for by in range(GY):
        slots.append((here, own(nb_ref[here, 14])))
        if by < GY - 1:
            here = own(nb_ref[here, 16])

    loads[1].wait()
    loads[2].wait()
    for b in range(BRICKS):
        occupied = occ_ref[b : b + 1, :].astype(jnp.float32)
        masked[b] = g_ref[b].astype(jnp.float32) * occupied
    for by in range(GY):
        even, odd = planes_of(masked[slots[by][0]], masked[slots[by][1]])
        at = slice(128 * by, 128 * (by + 1))
        for k in range(4):
            part = slice(128 * k, 128 * (k + 1))
            grads[1 + 2 * k, chan, :, at] = even[:, part].astype(jnp.bfloat16)
            grads[2 + 2 * k, chan, :, at] = odd[:, part].astype(jnp.bfloat16)

    zero_plane = jnp.zeros((2, 16, LANES), jnp.bfloat16)

    @pl.when(me == 0)
    def _():
        grads[0] = zero_plane

    @pl.when(me == count - 1)
    def _():
        grads[EDGE + 1] = zero_plane

    met = jnp.where(plain, PARTS, count - 1) + 1
    for more in (below, above, meet_below, meet_above):
        met = met + more.astype(jnp.int32)
    pl.semaphore_wait(barrier, met)

    def send_plane(source, target, index, core, k, channel):
        return pltpu.make_async_remote_copy(
            src_ref=grads.at[source, channel],
            dst_ref=grads.at[target, channel],
            send_sem=face_send.at[k],
            recv_sem=face_recv.at[k],
            device_id=place(index, core),
            device_id_type=MESH,
        )

    to_next = [
        send_plane(EDGE, 0, me + 1, chan, 1, chan),
        send_plane(EDGE, 0, me + 1, other, 2, chan),
    ]
    to_last = [
        send_plane(1, EDGE + 1, me - 1, chan, 3, chan),
        send_plane(1, EDGE + 1, me - 1, other, 4, chan),
    ]
    from_last = [
        send_plane(EDGE, 0, me - 1, chan, 1, chan),
        send_plane(EDGE, 0, me - 1, other, 2, other),
    ]
    from_next = [
        send_plane(1, EDGE + 1, me + 1, chan, 3, chan),
        send_plane(1, EDGE + 1, me + 1, other, 4, other),
    ]

    @pl.when(me < count - 1)
    def _():
        for copy in to_next:
            copy.start()

    @pl.when(me > 0)
    def _():
        for copy in to_last:
            copy.start()

    swap = send_plane(pl.ds(1, EDGE), pl.ds(1, EDGE), me, other, 0, chan)
    swap.start()
    swap_in = send_plane(pl.ds(1, EDGE), pl.ds(1, EDGE), me, other, 0, other)

    loads[3].wait()
    for b in range(BRICKS):
        occupied = occ_ref[b : b + 1, :].astype(jnp.float32)
        masked[b] = f_ref[b].astype(jnp.float32) * occupied
    for by in range(GY):
        even, odd = planes_of(masked[slots[by][0]], masked[slots[by][1]])
        at = slice(128 * by, 128 * (by + 1))
        for k in range(4):
            part = slice(128 * k, 128 * (k + 1))
            feats[2 * k, :, at] = even[:, part]
            feats[2 * k + 1, :, at] = odd[:, part]
    for x in range(EDGE):
        plane = feats[x]
        depth = jnp.concatenate([at_z(plane, -1), plane, at_z(plane, 1)], axis=0)
        shifted[x, 0:48] = at_y(depth, -1).astype(jnp.bfloat16)
        shifted[x, 48:96] = depth.astype(jnp.bfloat16)
        shifted[x, 96:144] = at_y(depth, 1).astype(jnp.bfloat16)
    loads[4].wait()
    for a in range(3):
        weights[:, 32 * a : 32 * (a + 1)] = w_ref[9 * a : 9 * (a + 1)].reshape(144, 32)

    def window(x):
        return jnp.concatenate(
            [grads[x + 2 - a].reshape(32, LANES) for a in range(3)], axis=0
        )

    def term(x):
        return lax.dot_general(
            shifted[x],
            window(x),
            (((1,), (1,)), ((), ())),
            preferred_element_type=jnp.float32,
        )

    swap_in.wait_recv()
    total = term(1)
    for x in range(2, EDGE - 1):
        total = total + term(x)

    @pl.when(me > 0)
    def _():
        for copy in from_last:
            copy.wait_recv()

    @pl.when(me < count - 1)
    def _():
        for copy in from_next:
            copy.wait_recv()

    total = total + term(0) + term(EDGE - 1)
    for q in range(PARTS):
        part = total[PART_ROWS * q : PART_ROWS * (q + 1)]
        terms[q, 0 : part.shape[0]] = part

    def give(q, source):
        return pltpu.make_async_remote_copy(
            src_ref=terms.at[q],
            dst_ref=arrived.at[source],
            send_sem=part_send.at[q],
            recv_sem=part_recv.at[source],
            device_id=place(first + q, chan),
            device_id_type=MESH,
        )

    for q in range(PARTS):

        @pl.when(me != first + q)
        def _():
            give(q, me).start()

    for x in range(EDGE):
        taps = jnp.dot(weights[...], window(x), preferred_element_type=jnp.float32)
        depth = taps[48:96] + at_y(taps[0:48], 1) + at_y(taps[96:144], -1)
        feats[x] = depth[16:32] + at_z(depth[0:16], 1) + at_z(depth[32:48], -1)
    for by in range(GY):
        at = slice(128 * by, 128 * (by + 1))
        even = jnp.concatenate([feats[2 * k, :, at] for k in range(4)], axis=1)
        odd = jnp.concatenate([feats[2 * k + 1, :, at] for k in range(4)], axis=1)
        rows[GZ * by], rows[GZ * by + 1] = planes_of(even, odd)
    for b in range(BRICKS):
        left = nb_ref[b, 10]
        next_left = nb_ref[own(left), 10]
        y = jnp.where(
            left < 0,
            0,
            jnp.where(next_left < 0, 1, jnp.where(nb_ref[b, 16] >= 0, 2, 3)),
        )
        z = jnp.where(nb_ref[b, 12] >= 0, 1, 0)
        occupied = occ_ref[b : b + 1, :].astype(jnp.float32)
        gf_ref[b] = (rows[GZ * y + z] * occupied).astype(jnp.bfloat16)

    gf_store = pltpu.make_async_copy(gf_ref, gf_out, store_sem.at[0])
    gf_store.start()

    def share(owner, target):
        return pltpu.make_async_remote_copy(
            src_ref=totals.at[owner],
            dst_ref=totals.at[owner],
            send_sem=total_send.at[target],
            recv_sem=total_recv.at[owner],
            device_id=place(target, chan),
            device_id_type=MESH,
        )

    mine = me - first

    @pl.when(owns(me))
    def _():
        each_peer(lambda peer, j: give(mine, peer).wait_recv())
        arrived[me] = terms[mine]

        def add(j, carry):
            return carry + arrived[j]

        if count <= 8:
            result = arrived[0]
            for j in range(1, count):
                result = add(j, result)
        else:
            result = lax.fori_loop(1, count, add, arrived[0])
        totals[mine] = result * scale
        each_peer(lambda peer, j: share(mine, peer).start())

    for q in range(PARTS):

        @pl.when(me != first + q)
        def _():
            share(q, first + q).wait_recv()

    whole = totals[...].reshape(PARTS * PART_ROWS, 96)[0:144]
    for a in range(3):
        gw_ref[9 * a : 9 * (a + 1)] = whole[:, 32 * a : 32 * (a + 1)].reshape(9, 16, 32)
    gw_store = pltpu.make_async_copy(gw_ref, gw_out, store_sem.at[1])
    gw_store.start()

    @pl.when(owns(me))
    def _():
        each_peer(lambda peer, j: share(mine, peer).wait_send())

    for q in range(PARTS):

        @pl.when(me != first + q)
        def _():
            give(q, me).wait_send()

    swap.wait_send()

    @pl.when(me < count - 1)
    def _():
        for copy in to_next:
            copy.wait_send()

    @pl.when(me > 0)
    def _():
        for copy in to_last:
            copy.wait_send()

    gf_store.wait()
    gw_store.wait()


def deliver(gf_in, gw_in, gf_out, gw_out, gf_ref, gw_ref, sem):
    steps = ((gf_in, gf_ref, gf_out), (gw_in, gw_ref, gw_out))
    loads = [
        pltpu.make_async_copy(source, held, sem.at[0, k])
        for k, (source, held, _) in enumerate(steps)
    ]
    stores = [
        pltpu.make_async_copy(held, target, sem.at[1, k])
        for k, (_, held, target) in enumerate(steps)
    ]
    for load in loads:
        load.start()
    for load, store in zip(loads, stores):
        load.wait()
        store.start()
    for store in stores:
        store.wait()


def local(features, out_grad, weight, occupancy, neighbours):
    count = lax.axis_size(LINE)
    scale = 1.0 / math.sqrt(features.shape[0] * count * LANES)
    part = (PART_ROWS, 96)
    hbm = pl.BlockSpec(memory_space=pltpu.HBM)
    outs = (
        jax.ShapeDtypeStruct(features.shape, jnp.bfloat16),
        jax.ShapeDtypeStruct(weight.shape, jnp.float32),
    )
    limit = 60 * 1024 * 1024

    def body(*refs):
        kernel(scale, *refs)

    results = pl.pallas_call(
        body,
        out_shape=outs,
        in_specs=[hbm] * 5,
        out_specs=(hbm, hbm),
        scratch_shapes=[
            pltpu.VMEM(features.shape, jnp.bfloat16),
            pltpu.VMEM(weight.shape, jnp.float32),
            pltpu.SemaphoreType.DMA((2,)),
            pltpu.VMEM(features.shape, jnp.bfloat16),
            pltpu.VMEM(out_grad.shape, jnp.bfloat16),
            pltpu.VMEM(weight.shape, jnp.bfloat16),
            pltpu.VMEM(occupancy.shape, jnp.int32),
            pltpu.SMEM(neighbours.shape, jnp.int32),
            pltpu.SemaphoreType.DMA((5,)),
            pltpu.VMEM((EDGE + 2, 2, 16, LANES), jnp.bfloat16),
            pltpu.VMEM((BRICKS, 16, LANES), jnp.float32),
            pltpu.VMEM((EDGE, 16, LANES), jnp.float32),
            pltpu.VMEM((EDGE, 144, LANES), jnp.bfloat16),
            pltpu.VMEM((144, 96), jnp.bfloat16),
            pltpu.VMEM((BRICKS, 16, LANES), jnp.float32),
            pltpu.VMEM((PARTS,) + part, jnp.float32),
            pltpu.VMEM((count,) + part, jnp.float32),
            pltpu.VMEM((PARTS,) + part, jnp.float32),
            pltpu.SemaphoreType.DMA((5,)),
            pltpu.SemaphoreType.DMA((5,)),
            pltpu.SemaphoreType.DMA((PARTS,)),
            pltpu.SemaphoreType.DMA((count,)),
            pltpu.SemaphoreType.DMA((count,)),
            pltpu.SemaphoreType.DMA((PARTS,)),
        ],
        compiler_params=pltpu.CompilerParams(
            collective_id=0, has_side_effects=True, vmem_limit_bytes=limit
        ),
        name="brick_conv_backward",
    )(features, out_grad, weight, occupancy, neighbours)
    return pl.pallas_call(
        deliver,
        out_shape=outs,
        in_specs=[hbm, hbm],
        out_specs=(hbm, hbm),
        scratch_shapes=[
            pltpu.VMEM(features.shape, jnp.bfloat16),
            pltpu.VMEM(weight.shape, jnp.float32),
            pltpu.SemaphoreType.DMA((2, 2)),
        ],
        compiler_params=pltpu.CompilerParams(vmem_limit_bytes=limit),
        name="deliver",
    )(*results)


def solution(mesh):
    rows = P(("groups", "region", "strip"), "chan", None)
    tables = P(("groups", "region", "strip"), None)
    return jax.shard_map(
        local,
        mesh=mesh,
        in_specs=(rows, rows, P(None, "chan", None), tables, tables),
        out_specs=(rows, P("groups", "chan", None)),
        check_vma=False,
    )
```

```python
import math

import jax
import jax.numpy as jnp
from jax import lax
from jax.experimental import pallas as pl
from jax.experimental.pallas import tpu as pltpu
from jax.sharding import PartitionSpec as P

GY = 4
GZ = 2
BRICKS = GY * GZ
EDGE = 8
LANES = 512
PARTS = 4
PART_ROWS = 40
MESH = pl.DeviceIdType.MESH
LINE = ("region", "strip")


def lane_of(shape):
    return lax.broadcasted_iota(jnp.int32, shape, len(shape) - 1)


def roll(a, distance):
    return pltpu.roll(a, distance % LANES, 1)


def at_y(a, step):
    lane = lane_of(a.shape)
    row = (lane // 8) % 8
    brick = lane // 128
    if step > 0:
        near, far, other = row < 7, brick < GY - 1, 72
    else:
        near, far, other = row > 0, brick > 0, 72
    return jnp.where(
        near,
        roll(a, -8 * step),
        jnp.where(far, roll(a, -other * step), jnp.zeros_like(a)),
    )


def at_z(a, step):
    lane = lane_of(a.shape)
    column = lane % 8
    brick = (lane // 64) % 2
    if step > 0:
        near, far = column < 7, brick == 0
    else:
        near, far = column > 0, brick == 1
    return jnp.where(
        near,
        roll(a, -step),
        jnp.where(far, roll(a, -57 * step), jnp.zeros_like(a)),
    )


def planes_of(first, second):
    low = lane_of(first.shape) % 128 < 64
    even = jnp.where(low, first, roll(second, 64))
    odd = jnp.where(low, roll(first, -64), second)
    return even, odd


def kernel(
    scale,
    f_in,
    g_in,
    w_in,
    occ_in,
    nb_in,
    gf_out,
    sum_out,
    gf_ref,
    store_sem,
    f_ref,
    g_ref,
    w_ref,
    occ_ref,
    nb_ref,
    load_sem,
    grads,
    masked,
    feats,
    shifted,
    weights,
    rows,
    terms,
    arrived,
    totals,
    face_send,
    face_recv,
    part_send,
    part_recv,
    total_send,
    total_recv,
):
    strips = lax.axis_size("strip")
    count = strips * lax.axis_size("region")
    chan = lax.axis_index("chan")
    me = lax.axis_index("region") * strips + lax.axis_index("strip")
    other = 1 - chan
    first = (count - PARTS) // 2

    def owns(index):
        return (index >= first) & (index < first + PARTS)

    def place(index, core):
        return {
            "region": lax.div(index, strips),
            "strip": lax.rem(index, strips),
            "chan": core,
        }

    def each_peer(body):
        if count <= 8:
            for j in range(1, count):
                body(lax.rem(me + j, count), j)
        else:

            def step(j, carry):
                body(lax.rem(me + j, count), j)
                return carry

            lax.fori_loop(1, count, step, 0)

    barrier = pltpu.get_barrier_semaphore()

    def greet(index, core):
        pl.semaphore_signal(
            barrier, inc=1, device_id=place(index, core), device_id_type=MESH
        )

    below, above = me > 0, me < count - 1
    plain = jnp.logical_not(owns(me))
    meet_below = below & plain & jnp.logical_not(owns(me - 1))
    meet_above = above & plain & jnp.logical_not(owns(me + 1))

    @pl.when(owns(me))
    def _():
        each_peer(lambda peer, j: greet(peer, chan))

    @pl.when(plain)
    def _():
        for q in range(PARTS):
            greet(first + q, chan)

    @pl.when(meet_below)
    def _():
        greet(me - 1, chan)

    @pl.when(meet_above)
    def _():
        greet(me + 1, chan)

    @pl.when(below)
    def _():
        greet(me - 1, other)

    @pl.when(above)
    def _():
        greet(me + 1, other)

    greet(me, other)

    pairs = (
        (nb_in, nb_ref),
        (occ_in, occ_ref),
        (g_in, g_ref),
        (f_in, f_ref),
        (w_in, w_ref),
    )
    loads = [
        pltpu.make_async_copy(source, target, load_sem.at[k])
        for k, (source, target) in enumerate(pairs)
    ]
    for load in loads:
        load.start()

    base = me * BRICKS

    def own(entry):
        return jnp.clip(entry - base, 0, BRICKS - 1)

    loads[0].wait()
    corner = 0
    for b in range(BRICKS):
        corner += jnp.where((nb_ref[b, 10] < 0) & (nb_ref[b, 12] < 0), b, 0)
    slots = []
    here = corner
    for by in range(GY):
        slots.append((here, own(nb_ref[here, 14])))
        if by < GY - 1:
            here = own(nb_ref[here, 16])

    loads[1].wait()
    loads[2].wait()
    for b in range(BRICKS):
        occupied = occ_ref[b : b + 1, :].astype(jnp.float32)
        masked[b] = g_ref[b].astype(jnp.float32) * occupied
    for by in range(GY):
        even, odd = planes_of(masked[slots[by][0]], masked[slots[by][1]])
        at = slice(128 * by, 128 * (by + 1))
        for k in range(4):
            part = slice(128 * k, 128 * (k + 1))
            grads[1 + 2 * k, chan, :, at] = even[:, part].astype(jnp.bfloat16)
            grads[2 + 2 * k, chan, :, at] = odd[:, part].astype(jnp.bfloat16)

    zero_plane = jnp.zeros((2, 16, LANES), jnp.bfloat16)

    @pl.when(me == 0)
    def _():
        grads[0] = zero_plane

    @pl.when(me == count - 1)
    def _():
        grads[EDGE + 1] = zero_plane

    met = jnp.where(plain, PARTS, count - 1) + 1
    for more in (below, above, meet_below, meet_above):
        met = met + more.astype(jnp.int32)
    pl.semaphore_wait(barrier, met)

    def send_plane(source, target, index, core, k, channel):
        return pltpu.make_async_remote_copy(
            src_ref=grads.at[source, channel],
            dst_ref=grads.at[target, channel],
            send_sem=face_send.at[k],
            recv_sem=face_recv.at[k],
            device_id=place(index, core),
            device_id_type=MESH,
        )

    to_next = [
        send_plane(EDGE, 0, me + 1, chan, 1, chan),
        send_plane(EDGE, 0, me + 1, other, 2, chan),
    ]
    to_last = [
        send_plane(1, EDGE + 1, me - 1, chan, 3, chan),
        send_plane(1, EDGE + 1, me - 1, other, 4, chan),
    ]
    from_last = [
        send_plane(EDGE, 0, me - 1, chan, 1, chan),
        send_plane(EDGE, 0, me - 1, other, 2, other),
    ]
    from_next = [
        send_plane(1, EDGE + 1, me + 1, chan, 3, chan),
        send_plane(1, EDGE + 1, me + 1, other, 4, other),
    ]

    @pl.when(me < count - 1)
    def _():
        for copy in to_next:
            copy.start()

    @pl.when(me > 0)
    def _():
        for copy in to_last:
            copy.start()

    swap = send_plane(pl.ds(1, EDGE), pl.ds(1, EDGE), me, other, 0, chan)
    swap.start()
    swap_in = send_plane(pl.ds(1, EDGE), pl.ds(1, EDGE), me, other, 0, other)

    loads[3].wait()
    for b in range(BRICKS):
        occupied = occ_ref[b : b + 1, :].astype(jnp.float32)
        masked[b] = f_ref[b].astype(jnp.float32) * occupied
    for by in range(GY):
        even, odd = planes_of(masked[slots[by][0]], masked[slots[by][1]])
        at = slice(128 * by, 128 * (by + 1))
        for k in range(4):
            part = slice(128 * k, 128 * (k + 1))
            feats[2 * k, :, at] = even[:, part]
            feats[2 * k + 1, :, at] = odd[:, part]
    for x in range(EDGE):
        plane = feats[x]
        depth = jnp.concatenate([at_z(plane, -1), plane, at_z(plane, 1)], axis=0)
        shifted[x, 0:48] = at_y(depth, -1).astype(jnp.bfloat16)
        shifted[x, 48:96] = depth.astype(jnp.bfloat16)
        shifted[x, 96:144] = at_y(depth, 1).astype(jnp.bfloat16)
    loads[4].wait()
    for a in range(3):
        weights[:, 32 * a : 32 * (a + 1)] = w_ref[9 * a : 9 * (a + 1)].reshape(144, 32)

    def window(x):
        return jnp.concatenate(
            [grads[x + 2 - a].reshape(32, LANES) for a in range(3)], axis=0
        )

    def term(x):
        return lax.dot_general(
            shifted[x],
            window(x),
            (((1,), (1,)), ((), ())),
            preferred_element_type=jnp.float32,
        )

    swap_in.wait_recv()
    total = term(1)
    for x in range(2, EDGE - 1):
        total = total + term(x)

    @pl.when(me > 0)
    def _():
        for copy in from_last:
            copy.wait_recv()

    @pl.when(me < count - 1)
    def _():
        for copy in from_next:
            copy.wait_recv()

    total = total + term(0) + term(EDGE - 1)
    for q in range(PARTS):
        part = total[PART_ROWS * q : PART_ROWS * (q + 1)]
        terms[q, 0 : part.shape[0]] = part

    def give(q, source):
        return pltpu.make_async_remote_copy(
            src_ref=terms.at[q],
            dst_ref=arrived.at[source],
            send_sem=part_send.at[q],
            recv_sem=part_recv.at[source],
            device_id=place(first + q, chan),
            device_id_type=MESH,
        )

    for q in range(PARTS):

        @pl.when(me != first + q)
        def _():
            give(q, me).start()

    for x in range(EDGE):
        taps = jnp.dot(weights[...], window(x), preferred_element_type=jnp.float32)
        depth = taps[48:96] + at_y(taps[0:48], 1) + at_y(taps[96:144], -1)
        feats[x] = depth[16:32] + at_z(depth[0:16], 1) + at_z(depth[32:48], -1)
    for by in range(GY):
        at = slice(128 * by, 128 * (by + 1))
        even = jnp.concatenate([feats[2 * k, :, at] for k in range(4)], axis=1)
        odd = jnp.concatenate([feats[2 * k + 1, :, at] for k in range(4)], axis=1)
        rows[GZ * by], rows[GZ * by + 1] = planes_of(even, odd)
    for b in range(BRICKS):
        left = nb_ref[b, 10]
        next_left = nb_ref[own(left), 10]
        y = jnp.where(
            left < 0,
            0,
            jnp.where(next_left < 0, 1, jnp.where(nb_ref[b, 16] >= 0, 2, 3)),
        )
        z = jnp.where(nb_ref[b, 12] >= 0, 1, 0)
        occupied = occ_ref[b : b + 1, :].astype(jnp.float32)
        gf_ref[b] = (rows[GZ * y + z] * occupied).astype(jnp.bfloat16)

    gf_store = pltpu.make_async_copy(gf_ref, gf_out, store_sem.at[0])
    gf_store.start()

    def share(owner, target):
        return pltpu.make_async_remote_copy(
            src_ref=totals.at[owner],
            dst_ref=totals.at[owner],
            send_sem=total_send.at[target],
            recv_sem=total_recv.at[owner],
            device_id=place(target, chan),
            device_id_type=MESH,
        )

    mine = me - first

    @pl.when(owns(me))
    def _():
        each_peer(lambda peer, j: give(mine, peer).wait_recv())
        arrived[me] = terms[mine]

        def add(j, carry):
            return carry + arrived[j]

        if count <= 8:
            result = arrived[0]
            for j in range(1, count):
                result = add(j, result)
        else:
            result = lax.fori_loop(1, count, add, arrived[0])
        totals[mine] = result * scale
        each_peer(lambda peer, j: share(mine, peer).start())

    for q in range(PARTS):

        @pl.when(me != first + q)
        def _():
            share(q, first + q).wait_recv()

    sum_store = pltpu.make_async_copy(totals, sum_out, store_sem.at[1])
    sum_store.start()

    @pl.when(owns(me))
    def _():
        each_peer(lambda peer, j: share(mine, peer).wait_send())

    for q in range(PARTS):

        @pl.when(me != first + q)
        def _():
            give(q, me).wait_send()

    swap.wait_send()

    @pl.when(me < count - 1)
    def _():
        for copy in to_next:
            copy.wait_send()

    @pl.when(me > 0)
    def _():
        for copy in to_last:
            copy.wait_send()

    gf_store.wait()
    sum_store.wait()


def deliver(gf_in, sum_in, gf_out, gw_out, gf_ref, sum_ref, gw_ref, sem):
    gf_load = pltpu.make_async_copy(gf_in, gf_ref, sem.at[0])
    sum_load = pltpu.make_async_copy(sum_in, sum_ref, sem.at[1])
    gf_store = pltpu.make_async_copy(gf_ref, gf_out, sem.at[2])
    gw_store = pltpu.make_async_copy(gw_ref, gw_out, sem.at[3])
    sum_load.start()
    gf_load.start()
    sum_load.wait()
    whole = sum_ref[...].reshape(PARTS * PART_ROWS, 96)[0:144]
    for a in range(3):
        gw_ref[9 * a : 9 * (a + 1)] = whole[:, 32 * a : 32 * (a + 1)].reshape(9, 16, 32)
    gw_store.start()
    gf_load.wait()
    gf_store.start()
    gw_store.wait()
    gf_store.wait()


def local(features, out_grad, weight, occupancy, neighbours):
    count = lax.axis_size(LINE)
    scale = 1.0 / math.sqrt(features.shape[0] * count * LANES)
    part = (PART_ROWS, 96)
    hbm = pl.BlockSpec(memory_space=pltpu.HBM)
    outs = (
        jax.ShapeDtypeStruct(features.shape, jnp.bfloat16),
        jax.ShapeDtypeStruct(weight.shape, jnp.float32),
    )
    limit = 60 * 1024 * 1024

    def body(*refs):
        kernel(scale, *refs)

    results = pl.pallas_call(
        body,
        out_shape=(outs[0], jax.ShapeDtypeStruct((PARTS,) + part, jnp.float32)),
        in_specs=[hbm] * 5,
        out_specs=(hbm, hbm),
        scratch_shapes=[
            pltpu.VMEM(features.shape, jnp.bfloat16),
            pltpu.SemaphoreType.DMA((2,)),
            pltpu.VMEM(features.shape, jnp.bfloat16),
            pltpu.VMEM(out_grad.shape, jnp.bfloat16),
            pltpu.VMEM(weight.shape, jnp.bfloat16),
            pltpu.VMEM(occupancy.shape, jnp.int32),
            pltpu.SMEM(neighbours.shape, jnp.int32),
            pltpu.SemaphoreType.DMA((5,)),
            pltpu.VMEM((EDGE + 2, 2, 16, LANES), jnp.bfloat16),
            pltpu.VMEM((BRICKS, 16, LANES), jnp.float32),
            pltpu.VMEM((EDGE, 16, LANES), jnp.float32),
            pltpu.VMEM((EDGE, 144, LANES), jnp.bfloat16),
            pltpu.VMEM((144, 96), jnp.bfloat16),
            pltpu.VMEM((BRICKS, 16, LANES), jnp.float32),
            pltpu.VMEM((PARTS,) + part, jnp.float32),
            pltpu.VMEM((count,) + part, jnp.float32),
            pltpu.VMEM((PARTS,) + part, jnp.float32),
            pltpu.SemaphoreType.DMA((5,)),
            pltpu.SemaphoreType.DMA((5,)),
            pltpu.SemaphoreType.DMA((PARTS,)),
            pltpu.SemaphoreType.DMA((count,)),
            pltpu.SemaphoreType.DMA((count,)),
            pltpu.SemaphoreType.DMA((PARTS,)),
        ],
        compiler_params=pltpu.CompilerParams(
            collective_id=0, has_side_effects=True, vmem_limit_bytes=limit
        ),
        name="brick_conv_backward",
    )(features, out_grad, weight, occupancy, neighbours)
    return pl.pallas_call(
        deliver,
        out_shape=outs,
        in_specs=[hbm, hbm],
        out_specs=(hbm, hbm),
        scratch_shapes=[
            pltpu.VMEM(features.shape, jnp.bfloat16),
            pltpu.VMEM((PARTS,) + part, jnp.float32),
            pltpu.VMEM(weight.shape, jnp.float32),
            pltpu.SemaphoreType.DMA((4,)),
        ],
        compiler_params=pltpu.CompilerParams(vmem_limit_bytes=limit),
        name="deliver",
    )(*results)


def solution(mesh):
    rows = P(("groups", "region", "strip"), "chan", None)
    tables = P(("groups", "region", "strip"), None)
    return jax.shard_map(
        local,
        mesh=mesh,
        in_specs=(rows, rows, P(None, "chan", None), tables, tables),
        out_specs=(rows, P("groups", "chan", None)),
        check_vma=False,
    )
```

```python
import math

import jax
import jax.numpy as jnp
from jax import lax
from jax.experimental import pallas as pl
from jax.experimental.pallas import tpu as pltpu
from jax.sharding import PartitionSpec as P

GY = 4
GZ = 2
BRICKS = GY * GZ
EDGE = 8
LANES = 512
PARTS = 4
PART_ROWS = 40
MESH = pl.DeviceIdType.MESH
LINE = ("region", "strip")


def lane_of(shape):
    return lax.broadcasted_iota(jnp.int32, shape, len(shape) - 1)


def roll(a, distance):
    return pltpu.roll(a, distance % LANES, 1)


def at_y(a, step):
    lane = lane_of(a.shape)
    row = (lane // 8) % 8
    brick = lane // 128
    if step > 0:
        near, far, other = row < 7, brick < GY - 1, 72
    else:
        near, far, other = row > 0, brick > 0, 72
    return jnp.where(
        near,
        roll(a, -8 * step),
        jnp.where(far, roll(a, -other * step), jnp.zeros_like(a)),
    )


def at_z(a, step):
    lane = lane_of(a.shape)
    column = lane % 8
    brick = (lane // 64) % 2
    if step > 0:
        near, far = column < 7, brick == 0
    else:
        near, far = column > 0, brick == 1
    return jnp.where(
        near,
        roll(a, -step),
        jnp.where(far, roll(a, -57 * step), jnp.zeros_like(a)),
    )


def planes_of(first, second):
    low = lane_of(first.shape) % 128 < 64
    even = jnp.where(low, first, roll(second, 64))
    odd = jnp.where(low, roll(first, -64), second)
    return even, odd


def kernel(
    scale,
    f_in,
    g_in,
    w_in,
    occ_in,
    nb_in,
    gf_out,
    sum_out,
    gf_ref,
    store_sem,
    f_ref,
    g_ref,
    w_ref,
    occ_ref,
    nb_ref,
    load_sem,
    grads,
    masked,
    feats,
    shifted,
    weights,
    rows,
    terms,
    arrived,
    totals,
    face_send,
    face_recv,
    part_send,
    part_recv,
    total_send,
    total_recv,
):
    strips = lax.axis_size("strip")
    count = strips * lax.axis_size("region")
    chan = lax.axis_index("chan")
    me = lax.axis_index("region") * strips + lax.axis_index("strip")
    other = 1 - chan
    first = (count - PARTS) // 2

    def owns(index):
        return (index >= first) & (index < first + PARTS)

    def place(index, core):
        return {
            "region": lax.div(index, strips),
            "strip": lax.rem(index, strips),
            "chan": core,
        }

    def each_peer(body):
        if count <= 8:
            for j in range(1, count):
                body(lax.rem(me + j, count), j)
        else:

            def step(j, carry):
                body(lax.rem(me + j, count), j)
                return carry

            lax.fori_loop(1, count, step, 0)

    barrier = pltpu.get_barrier_semaphore()

    def greet(index, core):
        pl.semaphore_signal(
            barrier, inc=1, device_id=place(index, core), device_id_type=MESH
        )

    below, above = me > 0, me < count - 1
    @pl.when(owns(me))
    def _():
        each_peer(lambda peer, j: greet(peer, chan))

    tell_below = below & jnp.logical_not(owns(me))
    tell_above = above & jnp.logical_not(owns(me))

    @pl.when(tell_below)
    def _():
        greet(me - 1, chan)

    @pl.when(tell_above)
    def _():
        greet(me + 1, chan)

    @pl.when(below)
    def _():
        greet(me - 1, other)

    @pl.when(above)
    def _():
        greet(me + 1, other)

    greet(me, other)

    pairs = (
        (nb_in, nb_ref),
        (occ_in, occ_ref),
        (g_in, g_ref),
        (f_in, f_ref),
        (w_in, w_ref),
    )
    loads = [
        pltpu.make_async_copy(source, target, load_sem.at[k])
        for k, (source, target) in enumerate(pairs)
    ]
    for load in loads:
        load.start()

    base = me * BRICKS

    def own(entry):
        return jnp.clip(entry - base, 0, BRICKS - 1)

    loads[0].wait()
    corner = 0
    for b in range(BRICKS):
        corner += jnp.where((nb_ref[b, 10] < 0) & (nb_ref[b, 12] < 0), b, 0)
    slots = []
    here = corner
    for by in range(GY):
        slots.append((here, own(nb_ref[here, 14])))
        if by < GY - 1:
            here = own(nb_ref[here, 16])

    loads[1].wait()
    loads[2].wait()
    for b in range(BRICKS):
        occupied = occ_ref[b : b + 1, :].astype(jnp.float32)
        masked[b] = g_ref[b].astype(jnp.float32) * occupied
    for by in range(GY):
        even, odd = planes_of(masked[slots[by][0]], masked[slots[by][1]])
        at = slice(128 * by, 128 * (by + 1))
        for k in range(4):
            part = slice(128 * k, 128 * (k + 1))
            grads[1 + 2 * k, chan, :, at] = even[:, part].astype(jnp.bfloat16)
            grads[2 + 2 * k, chan, :, at] = odd[:, part].astype(jnp.bfloat16)

    zero_plane = jnp.zeros((2, 16, LANES), jnp.bfloat16)

    @pl.when(me == 0)
    def _():
        grads[0] = zero_plane

    @pl.when(me == count - 1)
    def _():
        grads[EDGE + 1] = zero_plane

    met = jnp.where(owns(me), PARTS - 1, PARTS) + 1
    hear_below = below & jnp.logical_not(owns(me - 1))
    hear_above = above & jnp.logical_not(owns(me + 1))
    for more in (below, above, hear_below, hear_above):
        met = met + more.astype(jnp.int32)
    pl.semaphore_wait(barrier, met)

    def send_plane(source, target, index, core, k, channel):
        return pltpu.make_async_remote_copy(
            src_ref=grads.at[source, channel],
            dst_ref=grads.at[target, channel],
            send_sem=face_send.at[k],
            recv_sem=face_recv.at[k],
            device_id=place(index, core),
            device_id_type=MESH,
        )

    to_next = [
        send_plane(EDGE, 0, me + 1, chan, 1, chan),
        send_plane(EDGE, 0, me + 1, other, 2, chan),
    ]
    to_last = [
        send_plane(1, EDGE + 1, me - 1, chan, 3, chan),
        send_plane(1, EDGE + 1, me - 1, other, 4, chan),
    ]
    from_last = [
        send_plane(EDGE, 0, me - 1, chan, 1, chan),
        send_plane(EDGE, 0, me - 1, other, 2, other),
    ]
    from_next = [
        send_plane(1, EDGE + 1, me + 1, chan, 3, chan),
        send_plane(1, EDGE + 1, me + 1, other, 4, other),
    ]

    @pl.when(me < count - 1)
    def _():
        for copy in to_next:
            copy.start()

    @pl.when(me > 0)
    def _():
        for copy in to_last:
            copy.start()

    swap = send_plane(pl.ds(1, EDGE), pl.ds(1, EDGE), me, other, 0, chan)
    swap.start()
    swap_in = send_plane(pl.ds(1, EDGE), pl.ds(1, EDGE), me, other, 0, other)

    loads[3].wait()
    for b in range(BRICKS):
        occupied = occ_ref[b : b + 1, :].astype(jnp.float32)
        masked[b] = f_ref[b].astype(jnp.float32) * occupied
    for by in range(GY):
        even, odd = planes_of(masked[slots[by][0]], masked[slots[by][1]])
        at = slice(128 * by, 128 * (by + 1))
        for k in range(4):
            part = slice(128 * k, 128 * (k + 1))
            feats[2 * k, :, at] = even[:, part]
            feats[2 * k + 1, :, at] = odd[:, part]
    for x in range(EDGE):
        plane = feats[x]
        depth = jnp.concatenate([at_z(plane, -1), plane, at_z(plane, 1)], axis=0)
        shifted[x, 0:48] = at_y(depth, -1).astype(jnp.bfloat16)
        shifted[x, 48:96] = depth.astype(jnp.bfloat16)
        shifted[x, 96:144] = at_y(depth, 1).astype(jnp.bfloat16)
    loads[4].wait()
    for a in range(3):
        weights[:, 32 * a : 32 * (a + 1)] = w_ref[9 * a : 9 * (a + 1)].reshape(144, 32)

    def window(x):
        return jnp.concatenate(
            [grads[x + 2 - a].reshape(32, LANES) for a in range(3)], axis=0
        )

    def term(x):
        return lax.dot_general(
            shifted[x],
            window(x),
            (((1,), (1,)), ((), ())),
            preferred_element_type=jnp.float32,
        )

    swap_in.wait_recv()
    total = term(1)
    for x in range(2, EDGE - 1):
        total = total + term(x)

    @pl.when(me > 0)
    def _():
        for copy in from_last:
            copy.wait_recv()

    @pl.when(me < count - 1)
    def _():
        for copy in from_next:
            copy.wait_recv()

    total = total + term(0) + term(EDGE - 1)
    for q in range(PARTS):
        part = total[PART_ROWS * q : PART_ROWS * (q + 1)]
        terms[q, 0 : part.shape[0]] = part

    def give(q, source):
        return pltpu.make_async_remote_copy(
            src_ref=terms.at[q],
            dst_ref=arrived.at[source],
            send_sem=part_send.at[q],
            recv_sem=part_recv.at[source],
            device_id=place(first + q, chan),
            device_id_type=MESH,
        )

    for q in range(PARTS):

        @pl.when(me != first + q)
        def _():
            give(q, me).start()

    for x in range(EDGE):
        taps = jnp.dot(weights[...], window(x), preferred_element_type=jnp.float32)
        depth = taps[48:96] + at_y(taps[0:48], 1) + at_y(taps[96:144], -1)
        feats[x] = depth[16:32] + at_z(depth[0:16], 1) + at_z(depth[32:48], -1)
    for by in range(GY):
        at = slice(128 * by, 128 * (by + 1))
        even = jnp.concatenate([feats[2 * k, :, at] for k in range(4)], axis=1)
        odd = jnp.concatenate([feats[2 * k + 1, :, at] for k in range(4)], axis=1)
        rows[GZ * by], rows[GZ * by + 1] = planes_of(even, odd)
    for b in range(BRICKS):
        left = nb_ref[b, 10]
        next_left = nb_ref[own(left), 10]
        y = jnp.where(
            left < 0,
            0,
            jnp.where(next_left < 0, 1, jnp.where(nb_ref[b, 16] >= 0, 2, 3)),
        )
        z = jnp.where(nb_ref[b, 12] >= 0, 1, 0)
        occupied = occ_ref[b : b + 1, :].astype(jnp.float32)
        gf_ref[b] = (rows[GZ * y + z] * occupied).astype(jnp.bfloat16)

    gf_store = pltpu.make_async_copy(gf_ref, gf_out, store_sem.at[0])
    gf_store.start()

    def share(owner, target):
        return pltpu.make_async_remote_copy(
            src_ref=totals.at[owner],
            dst_ref=totals.at[owner],
            send_sem=total_send.at[target],
            recv_sem=total_recv.at[owner],
            device_id=place(target, chan),
            device_id_type=MESH,
        )

    mine = me - first

    @pl.when(owns(me))
    def _():
        each_peer(lambda peer, j: give(mine, peer).wait_recv())
        arrived[me] = terms[mine]

        def add(j, carry):
            return carry + arrived[j]

        if count <= 8:
            result = arrived[0]
            for j in range(1, count):
                result = add(j, result)
        else:
            result = lax.fori_loop(1, count, add, arrived[0])
        totals[mine] = result * scale
        each_peer(lambda peer, j: share(mine, peer).start())

    for q in range(PARTS):

        @pl.when(me != first + q)
        def _():
            share(q, first + q).wait_recv()

    sum_store = pltpu.make_async_copy(totals, sum_out, store_sem.at[1])
    sum_store.start()

    @pl.when(owns(me))
    def _():
        each_peer(lambda peer, j: share(mine, peer).wait_send())

    for q in range(PARTS):

        @pl.when(me != first + q)
        def _():
            give(q, me).wait_send()

    swap.wait_send()

    @pl.when(me < count - 1)
    def _():
        for copy in to_next:
            copy.wait_send()

    @pl.when(me > 0)
    def _():
        for copy in to_last:
            copy.wait_send()

    gf_store.wait()
    sum_store.wait()


def deliver(gf_in, sum_in, gf_out, gw_out, gf_ref, sum_ref, gw_ref, sem):
    gf_load = pltpu.make_async_copy(gf_in, gf_ref, sem.at[0])
    sum_load = pltpu.make_async_copy(sum_in, sum_ref, sem.at[1])
    gf_store = pltpu.make_async_copy(gf_ref, gf_out, sem.at[2])
    gw_store = pltpu.make_async_copy(gw_ref, gw_out, sem.at[3])
    sum_load.start()
    gf_load.start()
    sum_load.wait()
    whole = sum_ref[...].reshape(PARTS * PART_ROWS, 96)[0:144]
    for a in range(3):
        gw_ref[9 * a : 9 * (a + 1)] = whole[:, 32 * a : 32 * (a + 1)].reshape(9, 16, 32)
    gw_store.start()
    gf_load.wait()
    gf_store.start()
    gw_store.wait()
    gf_store.wait()


def local(features, out_grad, weight, occupancy, neighbours):
    count = lax.axis_size(LINE)
    scale = 1.0 / math.sqrt(features.shape[0] * count * LANES)
    part = (PART_ROWS, 96)
    hbm = pl.BlockSpec(memory_space=pltpu.HBM)
    outs = (
        jax.ShapeDtypeStruct(features.shape, jnp.bfloat16),
        jax.ShapeDtypeStruct(weight.shape, jnp.float32),
    )
    limit = 60 * 1024 * 1024

    def body(*refs):
        kernel(scale, *refs)

    results = pl.pallas_call(
        body,
        out_shape=(outs[0], jax.ShapeDtypeStruct((PARTS,) + part, jnp.float32)),
        in_specs=[hbm] * 5,
        out_specs=(hbm, hbm),
        scratch_shapes=[
            pltpu.VMEM(features.shape, jnp.bfloat16),
            pltpu.SemaphoreType.DMA((2,)),
            pltpu.VMEM(features.shape, jnp.bfloat16),
            pltpu.VMEM(out_grad.shape, jnp.bfloat16),
            pltpu.VMEM(weight.shape, jnp.bfloat16),
            pltpu.VMEM(occupancy.shape, jnp.int32),
            pltpu.SMEM(neighbours.shape, jnp.int32),
            pltpu.SemaphoreType.DMA((5,)),
            pltpu.VMEM((EDGE + 2, 2, 16, LANES), jnp.bfloat16),
            pltpu.VMEM((BRICKS, 16, LANES), jnp.float32),
            pltpu.VMEM((EDGE, 16, LANES), jnp.float32),
            pltpu.VMEM((EDGE, 144, LANES), jnp.bfloat16),
            pltpu.VMEM((144, 96), jnp.bfloat16),
            pltpu.VMEM((BRICKS, 16, LANES), jnp.float32),
            pltpu.VMEM((PARTS,) + part, jnp.float32),
            pltpu.VMEM((count,) + part, jnp.float32),
            pltpu.VMEM((PARTS,) + part, jnp.float32),
            pltpu.SemaphoreType.DMA((5,)),
            pltpu.SemaphoreType.DMA((5,)),
            pltpu.SemaphoreType.DMA((PARTS,)),
            pltpu.SemaphoreType.DMA((count,)),
            pltpu.SemaphoreType.DMA((count,)),
            pltpu.SemaphoreType.DMA((PARTS,)),
        ],
        compiler_params=pltpu.CompilerParams(
            collective_id=0, has_side_effects=True, vmem_limit_bytes=limit
        ),
        name="brick_conv_backward",
    )(features, out_grad, weight, occupancy, neighbours)
    return pl.pallas_call(
        deliver,
        out_shape=outs,
        in_specs=[hbm, hbm],
        out_specs=(hbm, hbm),
        scratch_shapes=[
            pltpu.VMEM(features.shape, jnp.bfloat16),
            pltpu.VMEM((PARTS,) + part, jnp.float32),
            pltpu.VMEM(weight.shape, jnp.float32),
            pltpu.SemaphoreType.DMA((4,)),
        ],
        compiler_params=pltpu.CompilerParams(vmem_limit_bytes=limit),
        name="deliver",
    )(*results)


def solution(mesh):
    rows = P(("groups", "region", "strip"), "chan", None)
    tables = P(("groups", "region", "strip"), None)
    return jax.shard_map(
        local,
        mesh=mesh,
        in_specs=(rows, rows, P(None, "chan", None), tables, tables),
        out_specs=(rows, P("groups", "chan", None)),
        check_vma=False,
    )
```
